256 devices in a mesh: gx: 4 (over y_lo, core), gy: 4 (over x), gz: 16 (over y_hi, z).
Axes of the slice: x: 4, y: 4 (y_hi: 2, y_lo: 2; y = y_hi * 2 + y_lo), z: 8, core: 2. Of those that a mesh axis runs over, the one named last changes fastest.
Arguments:
- field: float32 [512, 1024, 1024], P('gz', 'gy', 'gx'), may hold values from -6 to 6
Outputs:
- picture: float32 [4, 1024, 1024], P(None, ('gy', 'gz'), 'gx')
The draws below stay inside these ranges and needn't reach their ends.
All inputs are finite; a program needn't handle non-finite values.
Results may differ from the reference program's by a relative error of at most 0.00002.
Values sent between devices are 32-bit elements; how exact they have to be, the bound alone decides.
No kernel may reach another device: no remote copies, remote signals or barrier semaphores. Data moves between devices by JAX's collectives and lax.ppermute only.
A program may use at most 128 MiB of HBM per device.

```python
import jax
import jax.numpy as jnp
from jax import lax

NX = 1024
NY = 1024
NZ = 512


def block_levels(own_key, shape, split, least, high):
    gain = 1.0
    for position, parts in split:
        heights = jax.random.uniform(jax.random.fold_in(jax.random.fold_in(own_key, 6), position), (parts,), jnp.float32, least / len(split), high / len(split))
        gain = gain * jnp.repeat(jnp.exp(heights), shape[position] // parts).reshape((-1,) + (1,) * (len(shape) - 1 - position))
    return gain


def normal_values(key, extent, scale, most, split=(), kind=jnp.bfloat16):
    result = scale * jax.random.normal(key, extent, jnp.float32)
    if split:
        result = result * block_levels(key, extent, split, -0.22, 0.18)
    return jnp.clip(result, -most, most).astype(kind)


def setup_inputs(seed: int = 0) -> dict:
    streams_of = jax.random.split(jax.random.key(seed), 2)
    field = normal_values(streams_of[0], (NZ, NY, NX), 1.0, 6.0, ((0, 16), (1, 4), (2, 4)), jnp.float32)
    return dict(field=field)


def sample_light(centre_slice, grad_x, grad_y, grad_z, density):
    squared = grad_x * grad_x + grad_y * grad_y + grad_z * grad_z
    shading = 0.25 + 0.75 * jnp.abs((grad_x + 2.0 * grad_y + 2.0 * grad_z) / 3.0) / jnp.sqrt(squared + 1.0)
    extinction = density * (1.0 + jnp.tanh(centre_slice)) * (0.2 + squared / (1.0 + squared))
    opacity = 1.0 - jnp.exp(-extinction)
    emitted = jnp.stack([jax.nn.sigmoid(2.0 * centre_slice) * shading, jnp.exp(-centre_slice * centre_slice) * shading, jax.nn.sigmoid(-2.0 * centre_slice) * shading])
    return (opacity, emitted)

def reference(field):
    density = 4.0 / NZ

    def march(depth_index, state_pair):
        colour_sum, transmit = state_pair
        index_here = jnp.asarray(depth_index).astype(jnp.int32)
        index_low = jnp.maximum(index_here - 1, 0).astype(jnp.int32)
        index_high = jnp.minimum(index_here + 1, NZ - 1).astype(jnp.int32)
        centre_slice = lax.dynamic_index_in_dim(field, index_here, 0, keepdims=False)
        lower_slice = jnp.where(index_here > 0, lax.dynamic_index_in_dim(field, index_low, 0, keepdims=False), jnp.float32(0.0))
        upper_slice = jnp.where(index_here < NZ - 1, lax.dynamic_index_in_dim(field, index_high, 0, keepdims=False), jnp.float32(0.0))
        padded_slice = jnp.pad(centre_slice, 1)
        grad_x = (padded_slice[1:-1, 2:] - padded_slice[1:-1, :-2]) * 0.5
        grad_y = (padded_slice[2:, 1:-1] - padded_slice[:-2, 1:-1]) * 0.5
        grad_z = (upper_slice - lower_slice) * 0.5
        opacity, emitted = sample_light(centre_slice, grad_x, grad_y, grad_z, density)
        colour_sum = colour_sum + (transmit * opacity)[None] * emitted
        transmit = transmit * (1.0 - opacity)
        return (colour_sum, transmit)
    start = (jnp.zeros((3, NY, NX), jnp.float32), jnp.ones((NY, NX), jnp.float32))
    colour_sum, transmit = lax.fori_loop(0, NZ, march, start)
    return jnp.concatenate([colour_sum, (1.0 - transmit)[None]], axis=0)
```

```python
import jax
import jax.numpy as jnp
from jax import lax
from jax.experimental import pallas as pl
from jax.experimental.pallas import tpu as pltpu
from jax.sharding import PartitionSpec as P

LOG2E = 1.4426950408889634
LANES = 128


def face_kernel(f_ref, left_ref, right_ref, low_ref, high_ref, packed):
    step = pl.program_id(0)
    lane = lax.broadcasted_iota(jnp.int32, (8, LANES), 1)

    @pl.when(step == 0)
    def _():
        packed[...] = jnp.zeros_like(packed)

    def tile(r, carry):
        rows = pl.ds(pl.multiple_of(r * 8, 8), 8)
        acc = pltpu.roll(packed[rows, :], LANES - 8, 1)
        for kk in range(8):
            first = f_ref[kk, rows, 0:LANES]
            last = f_ref[kk, rows, LANES : 2 * LANES]
            acc = jnp.where(lane == 24 + kk, pltpu.roll(first, 24 + kk, 1), acc)
            acc = jnp.where(lane == 56 + kk, pltpu.roll(last, 57 + kk, 1), acc)
        packed[rows, :] = acc
        return carry

    lax.fori_loop(0, 32, tile, 0, unroll=4)
    for kk in range(8):
        low_ref[pl.ds(kk, 1), :] = f_ref[kk, 0:1, :]
        high_ref[pl.ds(kk, 1), :] = f_ref[kk, 255:256, :]

    @pl.when(step == pl.num_programs(0) - 1)
    def _():
        turned = packed[...].T
        left_ref[...] = turned[0:32]
        right_ref[...] = turned[32:64]


def faces(field):
    depth, rows, cols = field.shape
    face = jax.ShapeDtypeStruct((depth, rows), jnp.float32)
    return pl.pallas_call(
        face_kernel,
        grid=(depth // 8,),
        in_specs=[pl.BlockSpec((8, rows, cols), lambda i: (i, 0, 0))],
        out_specs=[
            pl.BlockSpec((depth, rows), lambda i: (0, 0)),
            pl.BlockSpec((depth, rows), lambda i: (0, 0)),
            pl.BlockSpec((8, cols), lambda i: (i, 0)),
            pl.BlockSpec((8, cols), lambda i: (i, 0)),
        ],
        out_shape=[face] * 4,
        scratch_shapes=[pltpu.VMEM((rows, LANES), jnp.float32)],
        compiler_params=pltpu.CompilerParams(vmem_limit_bytes=32 * 1024 * 1024),
    )(field)


def march_kernel(
    density, f_ref, left_ref, right_ref, low_ref, high_ref, near_ref, far_ref, out_ref, buf, mix, side, sems
):
    depth = f_ref.shape[0]
    parts = 4
    part_rows = 256 // parts

    def copy(part, half):
        return pltpu.make_async_copy(
            f_ref.at[:, pl.ds(part * part_rows, part_rows), pl.ds(half * LANES, LANES)],
            buf.at[half, :, pl.ds(8 + part * part_rows, part_rows), :],
            sems.at[part * 2 + half],
        )

    for part in range(parts):
        for half in range(2):
            copy(part, half).start()

    mix[...] = jnp.zeros_like(mix)
    for k in range(depth):
        mix[pl.ds(2 * k, 1), :] = left_ref[pl.ds(k, 1), :]
        mix[pl.ds((2 * k + LANES - 1) % LANES, 1), :] = right_ref[pl.ds(k, 1), :]
    side[...] = mix[...].T
    for k in range(depth):
        for half in range(2):
            cols = pl.ds(half * LANES, LANES)
            buf[half, k, pl.ds(7, 1), :] = low_ref[pl.ds(k, 1), cols]
            buf[half, k, pl.ds(264, 1), :] = high_ref[pl.ds(k, 1), cols]

    lane = lax.broadcasted_iota(jnp.int32, (8, LANES), 1)
    is_first = lane == 0
    is_last = lane == LANES - 1
    ext_scale = 4.0 * density * LOG2E
    ext_base = 1.2 * density * LOG2E

    def tile(r, carry):
        base = pl.multiple_of(r * 8, 8)
        here = pl.ds(8 + base, 8)
        edge = side[pl.ds(base, 8), :]
        prev = [near_ref[pl.ds(base, 8), pl.ds(h * LANES, LANES)] for h in range(2)]
        cur = [buf[h, 0, here, :] for h in range(2)]
        through = [jnp.ones((8, LANES), jnp.float32)] * 2
        total = [jnp.zeros((8, LANES), jnp.float32)] * 2
        tilted = [jnp.zeros((8, LANES), jnp.float32)] * 2
        bell = [jnp.zeros((8, LANES), jnp.float32)] * 2
        for k in range(depth):
            if k + 1 < depth:
                nxt = [buf[h, k + 1, here, :] for h in range(2)]
            else:
                nxt = [far_ref[pl.ds(base, 8), pl.ds(h * LANES, LANES)] for h in range(2)]
            fwd = [pltpu.roll(c, LANES - 1, 1) for c in cur]
            bwd = [pltpu.roll(c, 1, 1) for c in cur]
            upper = [jnp.where(is_last, fwd[1], fwd[0]), jnp.where(is_last, edge, fwd[1])]
            lower = [jnp.where(is_first, edge, bwd[0]), jnp.where(is_first, bwd[0], bwd[1])]
            if k + 1 < depth:
                edge = pltpu.roll(edge, LANES - 2, 1)
            for h in range(2):
                f = cur[h]
                a = upper[h] - lower[h]
                b = buf[h, k, pl.ds(base + 9, 8), :] - buf[h, k, pl.ds(base + 7, 8), :]
                c = nxt[h] - prev[h]
                bc = b + c
                slope = jnp.abs(a + (bc + bc))
                inv = lax.rsqrt((a * a + b * b) + (c * c + 4.0))
                t = jnp.tanh(f)
                gauss = jnp.exp2(f * (f * -LOG2E))
                keep = jnp.exp2((1.0 + t) * (inv * inv * ext_scale - ext_base))
                after = through[h] * keep
                w = through[h] - after
                ws = w * (1.0 + slope * inv)
                through[h] = after
                total[h] = total[h] + ws
                tilted[h] = tilted[h] + ws * t
                bell[h] = bell[h] + ws * gauss
            prev, cur = cur, nxt
        band = r // 2
        rows = pl.ds(pl.multiple_of((r % 2) * 8, 8), 8)
        for h in range(2):
            cols = pl.ds(h * LANES, LANES)
            out_ref[band, 0, rows, cols] = total[h]
            out_ref[band, 1, rows, cols] = tilted[h]
            out_ref[band, 2, rows, cols] = bell[h]
            out_ref[band, 3, rows, cols] = through[h]
        return carry

    tiles = part_rows // 8
    for half in range(2):
        copy(0, half).wait()
    for part in range(parts):
        if part + 1 < parts:
            for half in range(2):
                copy(part + 1, half).wait()
        lax.fori_loop(part * tiles, (part + 1) * tiles, tile, 0)


def march(field, left, right, low, high, near, far, density):
    depth, rows, cols = field.shape
    bands = 16
    vmem = pl.BlockSpec(memory_space=pltpu.VMEM)

    def kernel(*refs):
        march_kernel(density, *refs)

    return pl.pallas_call(
        kernel,
        in_specs=[pl.BlockSpec(memory_space=pl.ANY)] + [vmem] * 6,
        out_specs=vmem,
        out_shape=jax.ShapeDtypeStruct((bands, 4, rows // bands, cols), jnp.float32),
        scratch_shapes=[
            pltpu.VMEM((2, depth, rows + 16, LANES), jnp.float32),
            pltpu.VMEM((LANES, rows), jnp.float32),
            pltpu.VMEM((rows, LANES), jnp.float32),
            pltpu.SemaphoreType.DMA((8,)),
        ],
        compiler_params=pltpu.CompilerParams(vmem_limit_bytes=40 * 1024 * 1024),
    )(field, left, right, low, high, near, far)


def blend_kernel(parts_ref, out_ref):
    through = jnp.ones(parts_ref.shape[2:], jnp.float32)
    sums = [jnp.zeros(parts_ref.shape[2:], jnp.float32)] * 3
    for d in range(parts_ref.shape[0]):
        for c in range(3):
            sums[c] = sums[c] + through * parts_ref[d, c]
        through = through * parts_ref[d, 3]
    out_ref[0] = (sums[0] + sums[1]) * 0.125
    out_ref[1] = sums[2] * 0.25
    out_ref[2] = (sums[0] - sums[1]) * 0.125
    out_ref[3] = 1.0 - through


def blend(parts):
    return pl.pallas_call(
        blend_kernel,
        out_shape=jax.ShapeDtypeStruct(parts.shape[1:], jnp.float32),
    )(parts)


def shift(block, axis, up):
    count = lax.axis_size(axis)
    pairs = [(i, i + 1) if up else (i + 1, i) for i in range(count - 1)]
    return lax.ppermute(block, axis, pairs)


def per_device(field):
    depth = field.shape[0]
    density = 4.0 / (depth * lax.axis_size("gz"))
    near = shift(field[depth - 1], "gz", True)
    far = shift(field[0], "gz", False)
    left, right, low, high = faces(field)
    before_x = shift(right, "gx", True)
    after_x = shift(left, "gx", False)
    before_y = shift(high, "gy", True)
    after_y = shift(low, "gy", False)
    parts = march(field, before_x, after_x, before_y, after_y, near, far, density)
    parts = lax.all_to_all(parts, "gz", split_axis=0, concat_axis=0, tiled=True)
    return blend(parts)


def solution(mesh):
    return jax.shard_map(
        per_device,
        mesh=mesh,
        in_specs=(P("gz", "gy", "gx"),),
        out_specs=P(None, ("gy", "gz"), "gx"),
        check_vma=False,
    )
```

```python
import jax
import jax.numpy as jnp
from jax import lax
from jax.experimental import pallas as pl
from jax.experimental.pallas import tpu as pltpu
from jax.sharding import PartitionSpec as P

LOG2E = 1.4426950408889634
LANES = 128


def face_kernel(f_ref, left_ref, right_ref, low_ref, high_ref, packed):
    step = pl.program_id(0)
    lane = lax.broadcasted_iota(jnp.int32, (8, LANES), 1)

    @pl.when(step == 0)
    def _():
        packed[...] = jnp.zeros_like(packed)

    def tile(r, carry):
        rows = pl.ds(pl.multiple_of(r * 8, 8), 8)
        acc = pltpu.roll(packed[rows, :], LANES - 8, 1)
        for kk in range(8):
            first = f_ref[kk, rows, 0:LANES]
            last = f_ref[kk, rows, LANES : 2 * LANES]
            acc = jnp.where(lane == 24 + kk, pltpu.roll(first, 24 + kk, 1), acc)
            acc = jnp.where(lane == 56 + kk, pltpu.roll(last, 57 + kk, 1), acc)
        packed[rows, :] = acc
        return carry

    lax.fori_loop(0, 32, tile, 0, unroll=4)
    for kk in range(8):
        low_ref[pl.ds(kk, 1), :] = f_ref[kk, 0:1, :]
        high_ref[pl.ds(kk, 1), :] = f_ref[kk, 255:256, :]

    @pl.when(step == pl.num_programs(0) - 1)
    def _():
        turned = packed[...].T
        left_ref[...] = turned[0:32]
        right_ref[...] = turned[32:64]


def faces(field):
    depth, rows, cols = field.shape
    face = jax.ShapeDtypeStruct((depth, rows), jnp.float32)
    return pl.pallas_call(
        face_kernel,
        grid=(depth // 8,),
        in_specs=[pl.BlockSpec((8, rows, cols), lambda i: (i, 0, 0))],
        out_specs=[
            pl.BlockSpec((depth, rows), lambda i: (0, 0)),
            pl.BlockSpec((depth, rows), lambda i: (0, 0)),
            pl.BlockSpec((8, cols), lambda i: (i, 0)),
            pl.BlockSpec((8, cols), lambda i: (i, 0)),
        ],
        out_shape=[face] * 4,
        scratch_shapes=[pltpu.VMEM((rows, LANES), jnp.float32)],
        compiler_params=pltpu.CompilerParams(vmem_limit_bytes=60 * 1024 * 1024),
    )(field)


def march_kernel(
    density, f_ref, left_ref, right_ref, low_ref, high_ref, near_ref, far_ref, out_ref, buf, mix, side, sems
):
    depth = f_ref.shape[0]
    parts = 4
    part_rows = 256 // parts

    def copy(part, half):
        return pltpu.make_async_copy(
            f_ref.at[:, pl.ds(part * part_rows, part_rows), pl.ds(half * LANES, LANES)],
            buf.at[half, :, pl.ds(8 + part * part_rows, part_rows), :],
            sems.at[part * 2 + half],
        )

    for part in range(parts):
        for half in range(2):
            copy(part, half).start()

    mix[...] = jnp.zeros_like(mix)
    for k in range(depth):
        mix[pl.ds(2 * k, 1), :] = left_ref[pl.ds(k, 1), :]
        mix[pl.ds((2 * k + LANES - 1) % LANES, 1), :] = right_ref[pl.ds(k, 1), :]
    side[...] = mix[...].T
    for k in range(depth):
        for half in range(2):
            cols = pl.ds(half * LANES, LANES)
            buf[half, k, pl.ds(7, 1), :] = low_ref[pl.ds(k, 1), cols]
            buf[half, k, pl.ds(264, 1), :] = high_ref[pl.ds(k, 1), cols]

    lane = lax.broadcasted_iota(jnp.int32, (8, LANES), 1)
    is_first = lane == 0
    is_last = lane == LANES - 1
    ext_scale = 4.0 * density * LOG2E
    ext_base = 1.2 * density * LOG2E

    def tile(r, carry):
        base = pl.multiple_of(r * 8, 8)
        here = pl.ds(8 + base, 8)
        packed = side[pl.ds(base, 8), :]
        prev = [near_ref[pl.ds(base, 8), pl.ds(h * LANES, LANES)] for h in range(2)]
        cur = [buf[h, 0, here, :] for h in range(2)]
        through = [jnp.ones((8, LANES), jnp.float32)] * 2
        total = [jnp.zeros((8, LANES), jnp.float32)] * 2
        tilted = [jnp.zeros((8, LANES), jnp.float32)] * 2
        bell = [jnp.zeros((8, LANES), jnp.float32)] * 2
        for k in range(depth):
            if k + 1 < depth:
                nxt = [buf[h, k + 1, here, :] for h in range(2)]
            else:
                nxt = [far_ref[pl.ds(base, 8), pl.ds(h * LANES, LANES)] for h in range(2)]
            fwd = [pltpu.roll(c, LANES - 1, 1) for c in cur]
            bwd = [pltpu.roll(c, 1, 1) for c in cur]
            edge = pltpu.roll(packed, LANES - 2 * k, 1) if k else packed
            upper = [jnp.where(is_last, fwd[1], fwd[0]), jnp.where(is_last, edge, fwd[1])]
            lower = [jnp.where(is_first, edge, bwd[0]), jnp.where(is_first, bwd[0], bwd[1])]
            for h in range(2):
                f = cur[h]
                a = upper[h] - lower[h]
                b = buf[h, k, pl.ds(base + 9, 8), :] - buf[h, k, pl.ds(base + 7, 8), :]
                c = nxt[h] - prev[h]
                bc = b + c
                slope = jnp.abs(a + (bc + bc))
                inv = lax.rsqrt((a * a + b * b) + (c * c + 4.0))
                t = jnp.tanh(f)
                gauss = jnp.exp2(f * (f * -LOG2E))
                keep = jnp.exp2((1.0 + t) * (inv * inv * ext_scale - ext_base))
                after = through[h] * keep
                w = through[h] - after
                ws = w * (1.0 + slope * inv)
                through[h] = after
                total[h] = total[h] + ws
                tilted[h] = tilted[h] + ws * t
                bell[h] = bell[h] + ws * gauss
            prev, cur = cur, nxt
        band = r // 2
        rows = pl.ds(pl.multiple_of((r % 2) * 8, 8), 8)
        for h in range(2):
            cols = pl.ds(h * LANES, LANES)
            out_ref[band, 0, rows, cols] = total[h]
            out_ref[band, 1, rows, cols] = tilted[h]
            out_ref[band, 2, rows, cols] = bell[h]
            out_ref[band, 3, rows, cols] = through[h]
        return carry

    tiles = part_rows // 8
    for half in range(2):
        copy(0, half).wait()
    for part in range(parts):
        if part + 1 < parts:
            for half in range(2):
                copy(part + 1, half).wait()
        lax.fori_loop(part * tiles, (part + 1) * tiles, tile, 0)


def march(field, left, right, low, high, near, far, density):
    depth, rows, cols = field.shape
    bands = 16
    vmem = pl.BlockSpec(memory_space=pltpu.VMEM)

    def kernel(*refs):
        march_kernel(density, *refs)

    return pl.pallas_call(
        kernel,
        in_specs=[pl.BlockSpec(memory_space=pl.ANY)] + [vmem] * 6,
        out_specs=vmem,
        out_shape=jax.ShapeDtypeStruct((bands, 4, rows // bands, cols), jnp.float32),
        scratch_shapes=[
            pltpu.VMEM((2, depth, rows + 16, LANES), jnp.float32),
            pltpu.VMEM((LANES, rows), jnp.float32),
            pltpu.VMEM((rows, LANES), jnp.float32),
            pltpu.SemaphoreType.DMA((8,)),
        ],
        compiler_params=pltpu.CompilerParams(vmem_limit_bytes=60 * 1024 * 1024),
    )(field, left, right, low, high, near, far)


def blend_kernel(parts_ref, out_ref):
    through = jnp.ones(parts_ref.shape[2:], jnp.float32)
    sums = [jnp.zeros(parts_ref.shape[2:], jnp.float32)] * 3
    for d in range(parts_ref.shape[0]):
        for c in range(3):
            sums[c] = sums[c] + through * parts_ref[d, c]
        through = through * parts_ref[d, 3]
    out_ref[0] = (sums[0] + sums[1]) * 0.125
    out_ref[1] = sums[2] * 0.25
    out_ref[2] = (sums[0] - sums[1]) * 0.125
    out_ref[3] = 1.0 - through


def blend(parts):
    return pl.pallas_call(
        blend_kernel,
        out_shape=jax.ShapeDtypeStruct(parts.shape[1:], jnp.float32),
    )(parts)


def shift(block, axis, up):
    count = lax.axis_size(axis)
    pairs = [(i, i + 1) if up else (i + 1, i) for i in range(count - 1)]
    return lax.ppermute(block, axis, pairs)


def per_device(field):
    depth = field.shape[0]
    density = 4.0 / (depth * lax.axis_size("gz"))
    near = shift(field[depth - 1], "gz", True)
    far = shift(field[0], "gz", False)
    left, right, low, high = faces(field)
    before_x = shift(right, "gx", True)
    after_x = shift(left, "gx", False)
    before_y = shift(high, "gy", True)
    after_y = shift(low, "gy", False)
    parts = march(field, before_x, after_x, before_y, after_y, near, far, density)
    parts = lax.all_to_all(parts, "gz", split_axis=0, concat_axis=0, tiled=True)
    return blend(parts)


def solution(mesh):
    return jax.shard_map(
        per_device,
        mesh=mesh,
        in_specs=(P("gz", "gy", "gx"),),
        out_specs=P(None, ("gy", "gz"), "gx"),
        check_vma=False,
    )
```

```python
import jax
import jax.numpy as jnp
from jax import lax
from jax.experimental import pallas as pl
from jax.experimental.pallas import tpu as pltpu
from jax.sharding import PartitionSpec as P

LOG2E = 1.4426950408889634
LANES = 128
PARTS = 8
FACE_LIMIT = 40 * 1024 * 1024
MARCH_LIMIT = 24 * 1024 * 1024


def is_even(axis):
    return lax.rem(lax.axis_index(axis), 2) == 0


def pick(even, yes, no):
    return jnp.where(jnp.broadcast_to(even, yes.shape), yes, no)


def face_kernel(f_ref, out_ref, x0_ref, x1_ref, y0_ref, y1_ref, z0_ref, z1_ref, packed, sems):
    depth, rows, cols = f_ref.shape
    part_rows = rows // PARTS
    lane = lax.broadcasted_iota(jnp.int32, (8, LANES), 1)

    def copy(part, half):
        span = pl.ds(pl.multiple_of(part * part_rows, 8), part_rows)
        return pltpu.make_async_copy(
            f_ref.at[:, span, pl.ds(half * LANES, LANES)], out_ref.at[half, :, span, :], sems.at[part * 2 + half]
        )

    for part in range(PARTS):
        for half in range(2):
            copy(part, half).start()

    def tile(r):
        here = pl.ds(pl.multiple_of(r * 8, 8), 8)
        acc = jnp.zeros((8, LANES), jnp.float32)
        for k in range(depth):
            first = pltpu.roll(out_ref[0, k, here, :], k, 1) if k else out_ref[0, k, here, :]
            last = pltpu.roll(out_ref[1, k, here, :], depth + k + 1, 1)
            acc = jnp.where(lane == k, first, acc)
            acc = jnp.where(lane == depth + k, last, acc)
        packed[here, :] = acc

    def step(part, carry):
        for half in range(2):
            copy(part, half).wait()
        for r in range(part_rows // 8):
            tile(part * (part_rows // 8) + r)
        return carry

    lax.fori_loop(0, PARTS, step, 0)
    even_x, even_y, even_z = is_even("gx"), is_even("gy"), is_even("gz")
    turned = packed[...].T
    left, right = turned[0:depth], turned[depth : 2 * depth]
    x0_ref[...] = pick(even_x, right, left)
    x1_ref[...] = pick(even_x, left, right)
    for half in range(2):
        for k in range(depth):
            low, high = out_ref[half, k, 0:1, :], out_ref[half, k, rows - 1 : rows, :]
            y0_ref[half, pl.ds(k, 1), :] = pick(even_y, high, low)
            y1_ref[half, pl.ds(k, 1), :] = pick(even_y, low, high)
        near, far = out_ref[half, 0], out_ref[half, depth - 1]
        z0_ref[half] = pick(even_z, far, near)
        z1_ref[half] = pick(even_z, near, far)


def faces(field):
    depth, rows, cols = field.shape
    vmem = pl.BlockSpec(memory_space=pltpu.VMEM)
    shapes = [(2, depth, rows, LANES)] + [(depth, rows)] * 2 + [(2, depth, LANES)] * 2 + [(2, rows, LANES)] * 2
    return pl.pallas_call(
        face_kernel,
        in_specs=[pl.BlockSpec(memory_space=pl.ANY)],
        out_specs=[vmem] * 7,
        out_shape=[jax.ShapeDtypeStruct(shape, jnp.float32) for shape in shapes],
        scratch_shapes=[pltpu.VMEM((rows, LANES), jnp.float32), pltpu.SemaphoreType.DMA((2 * PARTS,))],
        compiler_params=pltpu.CompilerParams(vmem_limit_bytes=FACE_LIMIT),
    )(field)


def march_kernel(density, f_ref, x0_ref, x1_ref, y0_ref, y1_ref, z0_ref, z1_ref, out_ref, rim, mix, side):
    depth, rows = f_ref.shape[1:3]
    even_x, even_y, even_z = is_even("gx"), is_even("gy"), is_even("gz")
    mix[...] = jnp.zeros_like(mix)
    for k in range(depth):
        first, second = x0_ref[pl.ds(k, 1), :], x1_ref[pl.ds(k, 1), :]
        mix[pl.ds(2 * k, 1), :] = pick(even_x, second, first)
        mix[pl.ds((2 * k + LANES - 1) % LANES, 1), :] = pick(even_x, first, second)
    side[...] = mix[...].T
    for half in range(2):
        for k in range(depth):
            first, second = y0_ref[half, pl.ds(k, 1), :], y1_ref[half, pl.ds(k, 1), :]
            rim[0, half, k, pl.ds(7, 1), :] = pick(even_y, second, first)
            rim[0, half, k, pl.ds(8, 16), :] = f_ref[half, k, pl.ds(0, 16), :]
            rim[1, half, k, pl.ds(0, 16), :] = f_ref[half, k, pl.ds(rows - 16, 16), :]
            rim[1, half, k, pl.ds(16, 1), :] = pick(even_y, first, second)

    lane = lax.broadcasted_iota(jnp.int32, (8, LANES), 1)
    is_first = lane == 0
    is_last = lane == LANES - 1
    ext_scale = 4.0 * density * LOG2E
    ext_base = 1.2 * density * LOG2E

    def tile(r, source, offset):
        base = pl.multiple_of(r * 8, 8)

        def load(half, k, up):
            return source[half, k, pl.ds(offset + up, 8), :]

        def depth_halo(half, yes, no):
            return pick(even_z, yes[half, pl.ds(base, 8), :], no[half, pl.ds(base, 8), :])

        packed = side[pl.ds(base, 8), :]
        prev = [depth_halo(h, z1_ref, z0_ref) for h in range(2)]
        cur = [load(h, 0, 0) for h in range(2)]
        through = [jnp.ones((8, LANES), jnp.float32)] * 2
        total = [jnp.zeros((8, LANES), jnp.float32)] * 2
        tilted = [jnp.zeros((8, LANES), jnp.float32)] * 2
        bell = [jnp.zeros((8, LANES), jnp.float32)] * 2
        for k in range(depth):
            if k + 1 < depth:
                nxt = [load(h, k + 1, 0) for h in range(2)]
            else:
                nxt = [depth_halo(h, z0_ref, z1_ref) for h in range(2)]
            edge = pltpu.roll(packed, LANES - 2 * k, 1) if k else packed
            fwd = [pltpu.roll(c, LANES - 1, 1) for c in cur]
            bwd = [pltpu.roll(c, 1, 1) for c in cur]
            upper = [jnp.where(is_last, fwd[1], fwd[0]), jnp.where(is_last, edge, fwd[1])]
            lower = [jnp.where(is_first, edge, bwd[0]), jnp.where(is_first, bwd[0], bwd[1])]
            for h in range(2):
                f = cur[h]
                a = upper[h] - lower[h]
                b = load(h, k, 1) - load(h, k, -1)
                c = nxt[h] - prev[h]
                bc = b + c
                slope = jnp.abs(a + (bc + bc))
                inv = lax.rsqrt((a * a + b * b) + (c * c + 4.0))
                t = jnp.tanh(f)
                gauss = jnp.exp2(f * (f * -LOG2E))
                keep = jnp.exp2((1.0 + t) * (inv * inv * ext_scale - ext_base))
                after = through[h] * keep
                w = through[h] - after
                ws = w * (1.0 + slope * inv)
                through[h] = after
                total[h] = total[h] + ws
                tilted[h] = tilted[h] + ws * t
                bell[h] = bell[h] + ws * gauss
            prev, cur = cur, nxt
        band = r // 2
        target = pl.ds(pl.multiple_of(lax.rem(r, 2) * 8, 8), 8)
        for h in range(2):
            cols = pl.ds(h * LANES, LANES)
            out_ref[band, 0, target, cols] = total[h]
            out_ref[band, 1, target, cols] = tilted[h]
            out_ref[band, 2, target, cols] = bell[h]
            out_ref[band, 3, target, cols] = through[h]

    def inner(r, carry):
        tile(r, f_ref, r * 8)
        return carry

    tile(jnp.int32(0), rim.at[0], 8)
    lax.fori_loop(1, rows // 8 - 1, inner, 0)
    tile(jnp.int32(rows // 8 - 1), rim.at[1], 8)


def march(halos, density):
    depth, rows = halos[0].shape[1:3]
    cols = 2 * LANES
    bands = 16
    vmem = pl.BlockSpec(memory_space=pltpu.VMEM)

    def kernel(*refs):
        march_kernel(density, *refs)

    return pl.pallas_call(
        kernel,
        in_specs=[vmem] * 7,
        out_specs=vmem,
        out_shape=jax.ShapeDtypeStruct((bands, 4, rows // bands, cols), jnp.float32),
        scratch_shapes=[
            pltpu.VMEM((2, 2, depth, 24, LANES), jnp.float32),
            pltpu.VMEM((LANES, rows), jnp.float32),
            pltpu.VMEM((rows, LANES), jnp.float32),
        ],
        compiler_params=pltpu.CompilerParams(vmem_limit_bytes=MARCH_LIMIT),
    )(*halos)


def blend_kernel(parts_ref, out_ref):
    through = jnp.ones(parts_ref.shape[2:], jnp.float32)
    sums = [jnp.zeros(parts_ref.shape[2:], jnp.float32)] * 3
    for d in range(parts_ref.shape[0]):
        for c in range(3):
            sums[c] = sums[c] + through * parts_ref[d, c]
        through = through * parts_ref[d, 3]
    out_ref[0] = (sums[0] + sums[1]) * 0.125
    out_ref[1] = sums[2] * 0.25
    out_ref[2] = (sums[0] - sums[1]) * 0.125
    out_ref[3] = 1.0 - through


def blend(parts):
    return pl.pallas_call(
        blend_kernel,
        out_shape=jax.ShapeDtypeStruct(parts.shape[1:], jnp.float32),
    )(parts)


def swap(block, axis, start):
    pairs = []
    for i in range(start, lax.axis_size(axis) - 1, 2):
        pairs += [(i, i + 1), (i + 1, i)]
    return lax.ppermute(block, axis, pairs)


def per_device(field):
    depth = field.shape[0]
    density = 4.0 / (depth * lax.axis_size("gz"))
    whole, x0, x1, y0, y1, z0, z1 = faces(field)
    z0, z1 = swap(z0, "gz", 0), swap(z1, "gz", 1)
    x0, x1 = swap(x0, "gx", 0), swap(x1, "gx", 1)
    y0, y1 = swap(y0, "gy", 0), swap(y1, "gy", 1)
    parts = march((whole, x0, x1, y0, y1, z0, z1), density)
    parts = lax.all_to_all(parts, "gz", split_axis=0, concat_axis=0, tiled=True)
    return blend(parts)


def solution(mesh):
    return jax.shard_map(
        per_device,
        mesh=mesh,
        in_specs=(P("gz", "gy", "gx"),),
        out_specs=P(None, ("gy", "gz"), "gx"),
        check_vma=False,
    )
```

```python
import jax
import jax.numpy as jnp
from jax import lax
from jax.experimental import pallas as pl
from jax.experimental.pallas import tpu as pltpu
from jax.sharding import PartitionSpec as P

LOG2E = 1.4426950408889634
LANES = 128
PARTS = 8
FACE_LIMIT = 40 * 1024 * 1024
MARCH_LIMIT = 24 * 1024 * 1024


def is_even(axis):
    return lax.rem(lax.axis_index(axis), 2) == 0


def at_end(axis):
    place = lax.axis_index(axis)
    return (place == 0) | (place == lax.axis_size(axis) - 1)


def drop(end, block):
    return jnp.where(jnp.broadcast_to(end, block.shape), 0.0, block)


def pick(even, yes, no):
    return jnp.where(jnp.broadcast_to(even, yes.shape), yes, no)


def face_kernel(f_ref, out_ref, x0_ref, x1_ref, y0_ref, y1_ref, z0_ref, z1_ref, packed, sems):
    depth, rows, cols = f_ref.shape
    part_rows = rows // PARTS
    lane = lax.broadcasted_iota(jnp.int32, (8, LANES), 1)

    def copy(part, half):
        span = pl.ds(pl.multiple_of(part * part_rows, 8), part_rows)
        return pltpu.make_async_copy(
            f_ref.at[:, span, pl.ds(half * LANES, LANES)], out_ref.at[half, :, span, :], sems.at[part * 2 + half]
        )

    for part in range(PARTS):
        for half in range(2):
            copy(part, half).start()

    def tile(r):
        here = pl.ds(pl.multiple_of(r * 8, 8), 8)
        acc = jnp.zeros((8, LANES), jnp.float32)
        for k in range(depth):
            first = pltpu.roll(out_ref[0, k, here, :], k, 1) if k else out_ref[0, k, here, :]
            last = pltpu.roll(out_ref[1, k, here, :], depth + k + 1, 1)
            acc = jnp.where(lane == k, first, acc)
            acc = jnp.where(lane == depth + k, last, acc)
        packed[here, :] = acc

    def step(part, carry):
        for half in range(2):
            copy(part, half).wait()
        for r in range(part_rows // 8):
            tile(part * (part_rows // 8) + r)
        return carry

    lax.fori_loop(0, PARTS, step, 0)
    even_x, even_y, even_z = is_even("gx"), is_even("gy"), is_even("gz")
    turned = packed[...].T
    left, right = turned[0:depth], turned[depth : 2 * depth]
    x0_ref[...] = pick(even_x, right, left)
    x1_ref[...] = pick(even_x, left, right)
    for half in range(2):
        for k in range(depth):
            low, high = out_ref[half, k, 0:1, :], out_ref[half, k, rows - 1 : rows, :]
            y0_ref[half, pl.ds(k, 1), :] = pick(even_y, high, low)
            y1_ref[half, pl.ds(k, 1), :] = pick(even_y, low, high)
        near, far = out_ref[half, 0], out_ref[half, depth - 1]
        z0_ref[half] = pick(even_z, far, near)
        z1_ref[half] = pick(even_z, near, far)


def faces(field):
    depth, rows, cols = field.shape
    vmem = pl.BlockSpec(memory_space=pltpu.VMEM)
    shapes = [(2, depth, rows, LANES)] + [(depth, rows)] * 2 + [(2, depth, LANES)] * 2 + [(2, rows, LANES)] * 2
    return pl.pallas_call(
        face_kernel,
        in_specs=[pl.BlockSpec(memory_space=pl.ANY)],
        out_specs=[vmem] * 7,
        out_shape=[jax.ShapeDtypeStruct(shape, jnp.float32) for shape in shapes],
        scratch_shapes=[pltpu.VMEM((rows, LANES), jnp.float32), pltpu.SemaphoreType.DMA((2 * PARTS,))],
        compiler_params=pltpu.CompilerParams(vmem_limit_bytes=FACE_LIMIT),
    )(field)


def march_kernel(density, f_ref, x0_ref, x1_ref, y0_ref, y1_ref, z0_ref, z1_ref, out_ref, rim, mix, side):
    depth, rows = f_ref.shape[1:3]
    even_x, even_y, even_z = is_even("gx"), is_even("gy"), is_even("gz")
    end_x, end_y, end_z = at_end("gx"), at_end("gy"), at_end("gz")
    mix[...] = jnp.zeros_like(mix)
    for k in range(depth):
        first, second = x0_ref[pl.ds(k, 1), :], drop(end_x, x1_ref[pl.ds(k, 1), :])
        mix[pl.ds(2 * k, 1), :] = pick(even_x, second, first)
        mix[pl.ds((2 * k + LANES - 1) % LANES, 1), :] = pick(even_x, first, second)
    side[...] = mix[...].T
    for half in range(2):
        for k in range(depth):
            first, second = y0_ref[half, pl.ds(k, 1), :], drop(end_y, y1_ref[half, pl.ds(k, 1), :])
            rim[0, half, k, pl.ds(7, 1), :] = pick(even_y, second, first)
            rim[0, half, k, pl.ds(8, 16), :] = f_ref[half, k, pl.ds(0, 16), :]
            rim[1, half, k, pl.ds(0, 16), :] = f_ref[half, k, pl.ds(rows - 16, 16), :]
            rim[1, half, k, pl.ds(16, 1), :] = pick(even_y, first, second)

    lane = lax.broadcasted_iota(jnp.int32, (8, LANES), 1)
    is_first = lane == 0
    is_last = lane == LANES - 1
    ext_scale = 4.0 * density * LOG2E
    ext_base = 1.2 * density * LOG2E

    def tile(r, source, offset):
        base = pl.multiple_of(r * 8, 8)

        def load(half, k, up):
            return source[half, k, pl.ds(offset + up, 8), :]

        def depth_halo(half, near):
            first = z0_ref[half, pl.ds(base, 8), :]
            second = drop(end_z, z1_ref[half, pl.ds(base, 8), :])
            return pick(even_z, second, first) if near else pick(even_z, first, second)

        packed = side[pl.ds(base, 8), :]
        prev = [depth_halo(h, True) for h in range(2)]
        cur = [load(h, 0, 0) for h in range(2)]
        through = [jnp.ones((8, LANES), jnp.float32)] * 2
        total = [jnp.zeros((8, LANES), jnp.float32)] * 2
        tilted = [jnp.zeros((8, LANES), jnp.float32)] * 2
        bell = [jnp.zeros((8, LANES), jnp.float32)] * 2
        for k in range(depth):
            if k + 1 < depth:
                nxt = [load(h, k + 1, 0) for h in range(2)]
            else:
                nxt = [depth_halo(h, False) for h in range(2)]
            edge = pltpu.roll(packed, LANES - 2 * k, 1) if k else packed
            fwd = [pltpu.roll(c, LANES - 1, 1) for c in cur]
            bwd = [pltpu.roll(c, 1, 1) for c in cur]
            upper = [jnp.where(is_last, fwd[1], fwd[0]), jnp.where(is_last, edge, fwd[1])]
            lower = [jnp.where(is_first, edge, bwd[0]), jnp.where(is_first, bwd[0], bwd[1])]
            for h in range(2):
                f = cur[h]
                a = upper[h] - lower[h]
                b = load(h, k, 1) - load(h, k, -1)
                c = nxt[h] - prev[h]
                bc = b + c
                slope = jnp.abs((bc + bc) + a)
                inv = lax.rsqrt(((c * c + b * b) + 4.0) + a * a)
                t = jnp.tanh(f)
                gauss = jnp.exp2(f * (f * -LOG2E))
                keep = jnp.exp2((1.0 + t) * (inv * inv * ext_scale - ext_base))
                after = through[h] * keep
                w = through[h] - after
                ws = w * (1.0 + slope * inv)
                through[h] = after
                total[h] = total[h] + ws
                tilted[h] = tilted[h] + ws * t
                bell[h] = bell[h] + ws * gauss
            prev, cur = cur, nxt
        band = r // 2
        target = pl.ds(pl.multiple_of(lax.rem(r, 2) * 8, 8), 8)
        for h in range(2):
            cols = pl.ds(h * LANES, LANES)
            out_ref[band, 0, target, cols] = total[h]
            out_ref[band, 1, target, cols] = tilted[h]
            out_ref[band, 2, target, cols] = bell[h]
            out_ref[band, 3, target, cols] = through[h]

    def inner(r, carry):
        tile(r, f_ref, r * 8)
        return carry

    tile(jnp.int32(0), rim.at[0], 8)
    lax.fori_loop(1, rows // 8 - 1, inner, 0, unroll=3)
    tile(jnp.int32(rows // 8 - 1), rim.at[1], 8)


def march(halos, density):
    depth, rows = halos[0].shape[1:3]
    cols = 2 * LANES
    bands = 16
    vmem = pl.BlockSpec(memory_space=pltpu.VMEM)

    def kernel(*refs):
        march_kernel(density, *refs)

    return pl.pallas_call(
        kernel,
        in_specs=[vmem] * 7,
        out_specs=vmem,
        out_shape=jax.ShapeDtypeStruct((bands, 4, rows // bands, cols), jnp.float32),
        scratch_shapes=[
            pltpu.VMEM((2, 2, depth, 24, LANES), jnp.float32),
            pltpu.VMEM((LANES, rows), jnp.float32),
            pltpu.VMEM((rows, LANES), jnp.float32),
        ],
        compiler_params=pltpu.CompilerParams(vmem_limit_bytes=MARCH_LIMIT),
    )(*halos)


def blend_kernel(parts_ref, out_ref):
    through = jnp.ones(parts_ref.shape[2:], jnp.float32)
    sums = [jnp.zeros(parts_ref.shape[2:], jnp.float32)] * 3
    for d in range(parts_ref.shape[0]):
        for c in range(3):
            sums[c] = sums[c] + through * parts_ref[d, c]
        through = through * parts_ref[d, 3]
    out_ref[0] = (sums[0] + sums[1]) * 0.125
    out_ref[1] = sums[2] * 0.25
    out_ref[2] = (sums[0] - sums[1]) * 0.125
    out_ref[3] = 1.0 - through


def blend(parts):
    return pl.pallas_call(
        blend_kernel,
        out_shape=jax.ShapeDtypeStruct(parts.shape[1:], jnp.float32),
    )(parts)


def swap(block, axis, start):
    count = lax.axis_size(axis)
    pairs = []
    for i in range(start, count, 2):
        pairs += [(i, (i + 1) % count), ((i + 1) % count, i)]
    return lax.ppermute(block, axis, pairs)


def per_device(field):
    depth = field.shape[0]
    density = 4.0 / (depth * lax.axis_size("gz"))
    whole, x0, x1, y0, y1, z0, z1 = faces(field)
    z0, z1 = swap(z0, "gz", 0), swap(z1, "gz", 1)
    x0, x1 = swap(x0, "gx", 0), swap(x1, "gx", 1)
    y0, y1 = swap(y0, "gy", 0), swap(y1, "gy", 1)
    parts = march((whole, x0, x1, y0, y1, z0, z1), density)
    parts = lax.all_to_all(parts, "gz", split_axis=0, concat_axis=0, tiled=True)
    return blend(parts)


def solution(mesh):
    return jax.shard_map(
        per_device,
        mesh=mesh,
        in_specs=(P("gz", "gy", "gx"),),
        out_specs=P(None, ("gy", "gz"), "gx"),
        check_vma=False,
    )
```

```python
import functools

import jax
import jax.numpy as jnp
from jax import lax
from jax.experimental import pallas as pl
from jax.experimental.pallas import tpu as pltpu
from jax.sharding import PartitionSpec as P

LOG2E = 1.4426950408889634
LANES = 128
BANDS = 16
PARTS = 8
FACE_LIMIT = 40 * 1024 * 1024
MARCH_LIMIT = 24 * 1024 * 1024


def is_even(axis):
    return lax.rem(lax.axis_index(axis), 2) == 0


def at_end(axis):
    place = lax.axis_index(axis)
    return (place == 0) | (place == lax.axis_size(axis) - 1)


def drop(end, block):
    return jnp.where(jnp.broadcast_to(end, block.shape), 0.0, block)


def pick(even, yes, no):
    return jnp.where(jnp.broadcast_to(even, yes.shape), yes, no)


def face_kernel(f_ref, out_ref, x0_ref, x1_ref, y0_ref, y1_ref, z0_ref, z1_ref, packed, sems):
    depth, rows, cols = f_ref.shape
    part_rows = rows // PARTS
    lane = lax.broadcasted_iota(jnp.int32, (8, LANES), 1)

    def copy(part, half):
        span = pl.ds(pl.multiple_of(part * part_rows, 8), part_rows)
        return pltpu.make_async_copy(
            f_ref.at[:, span, pl.ds(half * LANES, LANES)], out_ref.at[half, :, span, :], sems.at[part * 2 + half]
        )

    for part in range(PARTS):
        for half in range(2):
            copy(part, half).start()

    def tile(r):
        here = pl.ds(pl.multiple_of(r * 8, 8), 8)
        acc = jnp.zeros((8, LANES), jnp.float32)
        for k in range(depth):
            first = pltpu.roll(out_ref[0, k, here, :], k, 1) if k else out_ref[0, k, here, :]
            last = pltpu.roll(out_ref[1, k, here, :], depth + k + 1, 1)
            acc = jnp.where(lane == k, first, acc)
            acc = jnp.where(lane == depth + k, last, acc)
        packed[here, :] = acc

    def step(part, carry):
        for half in range(2):
            copy(part, half).wait()
        for r in range(part_rows // 8):
            tile(part * (part_rows // 8) + r)
        return carry

    lax.fori_loop(0, PARTS, step, 0)
    even_x, even_y, even_z = is_even("gx"), is_even("gy"), is_even("gz")
    turned = packed[...].T
    left, right = turned[0:depth], turned[depth : 2 * depth]
    x0_ref[...] = pick(even_x, right, left)
    x1_ref[...] = pick(even_x, left, right)
    for half in range(2):
        for k in range(depth):
            low, high = out_ref[half, k, 0:1, :], out_ref[half, k, rows - 1 : rows, :]
            y0_ref[half, pl.ds(k, 1), :] = pick(even_y, high, low)
            y1_ref[half, pl.ds(k, 1), :] = pick(even_y, low, high)
        near, far = out_ref[half, 0], out_ref[half, depth - 1]
        z0_ref[half] = pick(even_z, far, near)
        z1_ref[half] = pick(even_z, near, far)


def faces(field):
    depth, rows, cols = field.shape
    vmem = pl.BlockSpec(memory_space=pltpu.VMEM)
    shapes = [(2, depth, rows, LANES)] + [(depth, rows)] * 2 + [(2, depth, LANES)] * 2 + [(2, rows, LANES)] * 2
    return pl.pallas_call(
        face_kernel,
        in_specs=[pl.BlockSpec(memory_space=pl.ANY)],
        out_specs=[vmem] * 7,
        out_shape=[jax.ShapeDtypeStruct(shape, jnp.float32) for shape in shapes],
        scratch_shapes=[pltpu.VMEM((rows, LANES), jnp.float32), pltpu.SemaphoreType.DMA((2 * PARTS,))],
        compiler_params=pltpu.CompilerParams(vmem_limit_bytes=FACE_LIMIT),
    )(field)


def side_columns(x0_ref, x1_ref, mix, side_ref):
    depth = x0_ref.shape[0]
    even, end = is_even("gx"), at_end("gx")
    mix[...] = jnp.zeros_like(mix)
    for k in range(depth):
        first, second = x0_ref[pl.ds(k, 1), :], drop(end, x1_ref[pl.ds(k, 1), :])
        mix[pl.ds(2 * k, 1), :] = pick(even, second, first)
        mix[pl.ds((2 * k + LANES - 1) % LANES, 1), :] = pick(even, first, second)
    side_ref[...] = mix[...].T


def rim_rows(f_ref, y0_ref, y1_ref, rim):
    depth, rows = f_ref.shape[1:3]
    even, end = is_even("gy"), at_end("gy")
    for half in range(2):
        for k in range(depth):
            first, second = y0_ref[half, pl.ds(k, 1), :], drop(end, y1_ref[half, pl.ds(k, 1), :])
            rim[0, half, k, pl.ds(7, 1), :] = pick(even, second, first)
            rim[0, half, k, pl.ds(8, 16), :] = f_ref[half, k, pl.ds(0, 16), :]
            rim[1, half, k, pl.ds(0, 16), :] = f_ref[half, k, pl.ds(rows - 16, 16), :]
            rim[1, half, k, pl.ds(16, 1), :] = pick(even, first, second)


def march_tile(density, depth, r, source, offset, side_ref, z0_ref, z1_ref):
    base = pl.multiple_of(r * 8, 8)
    lane = lax.broadcasted_iota(jnp.int32, (8, LANES), 1)
    is_first = lane == 0
    is_last = lane == LANES - 1
    ext_scale = 4.0 * density * LOG2E
    ext_base = 1.2 * density * LOG2E
    even, end = is_even("gz"), at_end("gz")

    def load(half, k, up):
        return source[half, k, pl.ds(offset + up, 8), :]

    def depth_halo(half, near):
        first = z0_ref[half, pl.ds(base, 8), :]
        second = drop(end, z1_ref[half, pl.ds(base, 8), :])
        return pick(even, second, first) if near else pick(even, first, second)

    packed = side_ref[pl.ds(base, 8), :]
    prev = [depth_halo(h, True) for h in range(2)]
    cur = [load(h, 0, 0) for h in range(2)]
    through = [jnp.ones((8, LANES), jnp.float32)] * 2
    total = [jnp.zeros((8, LANES), jnp.float32)] * 2
    tilted = [jnp.zeros((8, LANES), jnp.float32)] * 2
    bell = [jnp.zeros((8, LANES), jnp.float32)] * 2
    for k in range(depth):
        if k + 1 < depth:
            nxt = [load(h, k + 1, 0) for h in range(2)]
        else:
            nxt = [depth_halo(h, False) for h in range(2)]
        edge = pltpu.roll(packed, LANES - 2 * k, 1) if k else packed
        fwd = [pltpu.roll(c, LANES - 1, 1) for c in cur]
        bwd = [pltpu.roll(c, 1, 1) for c in cur]
        upper = [jnp.where(is_last, fwd[1], fwd[0]), jnp.where(is_last, edge, fwd[1])]
        lower = [jnp.where(is_first, edge, bwd[0]), jnp.where(is_first, bwd[0], bwd[1])]
        for h in range(2):
            f = cur[h]
            a = upper[h] - lower[h]
            b = load(h, k, 1) - load(h, k, -1)
            c = nxt[h] - prev[h]
            bc = b + c
            slope = jnp.abs((bc + bc) + a)
            inv = lax.rsqrt(((c * c + b * b) + 4.0) + a * a)
            t = jnp.tanh(f)
            gauss = jnp.exp2(f * (f * -LOG2E))
            keep = jnp.exp2((1.0 + t) * (inv * inv * ext_scale - ext_base))
            after = through[h] * keep
            w = through[h] - after
            ws = w * (1.0 + slope * inv)
            through[h] = after
            total[h] = total[h] + ws
            tilted[h] = tilted[h] + ws * t
            bell[h] = bell[h] + ws * gauss
        prev, cur = cur, nxt
    return [(total[h], tilted[h], bell[h], through[h]) for h in range(2)]


def first_kernel(density, f_ref, x0_ref, x1_ref, y0_ref, y1_ref, z0_ref, z1_ref, keep_ref, send_ref, side_ref, mix):
    depth = f_ref.shape[1]
    side_columns(x0_ref, x1_ref, mix, side_ref)
    even = is_even("gz")

    def step(band, carry):
        r = jnp.where(band == 0, 1, 2 * band)
        halves = march_tile(density, depth, r, f_ref, pl.multiple_of(r * 8, 8), side_ref, z0_ref, z1_ref)
        for c, (left, right) in enumerate(zip(*halves)):
            keep_ref[band, c] = pick(even, left, right)
            send_ref[band, c] = pick(even, right, left)
        return carry

    lax.fori_loop(0, BANDS, step, 0, unroll=4)


def rest_kernel(density, f_ref, side_ref, y0_ref, y1_ref, z0_ref, z1_ref, out_ref, rim):
    depth, rows = f_ref.shape[1:3]
    rim_rows(f_ref, y0_ref, y1_ref, rim)

    def tile(band, r, source, offset):
        halves = march_tile(density, depth, r, source, offset, side_ref, z0_ref, z1_ref)
        for half in range(2):
            for c in range(4):
                out_ref[band, half + 1, c] = halves[half][c]

    def step(band, carry):
        r = 2 * band + 1
        tile(band, r, f_ref, pl.multiple_of(r * 8, 8))
        return carry

    tile(0, jnp.int32(0), rim.at[0], 8)
    lax.fori_loop(1, BANDS - 1, step, 0, unroll=7)
    tile(BANDS - 1, jnp.int32(rows // 8 - 1), rim.at[1], 8)


def merge_kernel(own_ref, other_ref, parts_ref, out_ref):
    even = is_even("gz")

    def step(band, carry):
        mine = [own_ref[band, c] for c in range(4)]
        theirs = [other_ref[band, c] for c in range(4)]
        near = [pick(even, m, t) for m, t in zip(mine, theirs)]
        far = [pick(even, t, m) for m, t in zip(mine, theirs)]
        for c in range(3):
            out_ref[band, 0, c] = near[c] + near[3] * far[c]
        out_ref[band, 0, 3] = near[3] * far[3]
        return carry

    lax.fori_loop(0, BANDS, step, 0, unroll=4)


def call(kernel, shapes, scratch, args, cells=0, aliases={}):
    vmem = pl.BlockSpec(memory_space=pltpu.VMEM)
    cost = pl.CostEstimate(flops=40 * cells, bytes_accessed=4 * cells, transcendentals=4 * cells) if cells else None
    return pl.pallas_call(
        kernel,
        in_specs=[vmem] * len(args),
        out_specs=[vmem] * len(shapes),
        out_shape=[jax.ShapeDtypeStruct(shape, jnp.float32) for shape in shapes],
        scratch_shapes=scratch,
        input_output_aliases=aliases,
        cost_estimate=cost,
        compiler_params=pltpu.CompilerParams(vmem_limit_bytes=MARCH_LIMIT),
    )(*args)


def blend_kernel(parts_ref, out_ref):
    lone = lax.axis_index("gz") == 0
    for block, half, ids in (
        (0, 0, range(0, BANDS, 2)),
        (0, 1, range(1, BANDS, 2)),
        (1, 0, range(BANDS)),
        (2, 1, range(BANDS)),
    ):
        through = jnp.ones((8, LANES), jnp.float32)
        sums = [jnp.zeros((8, LANES), jnp.float32) for c in range(3)]
        for d in ids:
            for c in range(3):
                sums[c] = sums[c] + through * parts_ref[d, block, c]
            through = through * parts_ref[d, block, 3]
        where = jnp.where(lone, 8, 0) if block == 0 else jnp.where(lone, 0, 8)
        rows = pl.ds(pl.multiple_of(where, 8), 8)
        cols = pl.ds(half * LANES, LANES)
        out_ref[0, rows, cols] = (sums[0] + sums[1]) * 0.125
        out_ref[1, rows, cols] = sums[2] * 0.25
        out_ref[2, rows, cols] = (sums[0] - sums[1]) * 0.125
        out_ref[3, rows, cols] = 1.0 - through


def blend(parts, cols):
    return pl.pallas_call(
        blend_kernel,
        out_shape=jax.ShapeDtypeStruct((4, 16, cols), jnp.float32),
    )(parts)


def swap(block, axis, start):
    count = lax.axis_size(axis)
    pairs = []
    for i in range(start, count, 2):
        pairs += [(i, (i + 1) % count), ((i + 1) % count, i)]
    return lax.ppermute(block, axis, pairs)


def per_device(field):
    depth = field.shape[0]
    density = 4.0 / (depth * lax.axis_size("gz"))
    whole, x0, x1, y0, y1, z0, z1 = faces(field)
    z0, z1 = swap(z0, "gz", 0), swap(z1, "gz", 1)
    x0, x1 = swap(x0, "gx", 0), swap(x1, "gx", 1)
    y0, y1 = swap(y0, "gy", 0), swap(y1, "gy", 1)
    cells = depth * BANDS * 8 * field.shape[2]
    block = (BANDS, 4, 8, LANES)
    own, sent, side = call(
        functools.partial(first_kernel, density),
        [block, block, (BANDS * 16, LANES)],
        [pltpu.VMEM((LANES, BANDS * 16), jnp.float32)],
        (whole, x0, x1, y0, y1, z0, z1),
        cells,
    )
    other = swap(sent, "gz", 0)
    (parts,) = call(
        functools.partial(rest_kernel, density),
        [(BANDS, 3, 4, 8, LANES)],
        [pltpu.VMEM((2, 2, depth, 24, LANES), jnp.float32)],
        (whole, side, y0, y1, z0, z1),
        cells,
    )
    (parts,) = call(merge_kernel, [parts.shape], [], (own, other, parts), aliases={2: 0})
    parts = lax.all_to_all(parts, "gz", split_axis=0, concat_axis=0, tiled=True)
    return blend(parts, field.shape[2])


def solution(mesh):
    return jax.shard_map(
        per_device,
        mesh=mesh,
        in_specs=(P("gz", "gy", "gx"),),
        out_specs=P(None, ("gy", "gz"), "gx"),
        check_vma=False,
    )
```

```python
import functools

import jax
import jax.numpy as jnp
from jax import lax
from jax.experimental import pallas as pl
from jax.experimental.pallas import tpu as pltpu
from jax.sharding import PartitionSpec as P

LOG2E = 1.4426950408889634
LANES = 128
BANDS = 16
PARTS = 8
FACE_LIMIT = 40 * 1024 * 1024
MARCH_LIMIT = 24 * 1024 * 1024


def is_even(axis):
    return lax.rem(lax.axis_index(axis), 2) == 0


def at_end(axis):
    place = lax.axis_index(axis)
    return (place == 0) | (place == lax.axis_size(axis) - 1)


def drop(end, block):
    return jnp.where(jnp.broadcast_to(end, block.shape), 0.0, block)


def pick(even, yes, no):
    return jnp.where(jnp.broadcast_to(even, yes.shape), yes, no)


def face_kernel(f_ref, out_ref, x0_ref, x1_ref, y0_ref, y1_ref, packed, sems):
    depth, rows, cols = f_ref.shape
    part_rows = rows // PARTS
    lane = lax.broadcasted_iota(jnp.int32, (8, LANES), 1)

    def copy(part, half):
        span = pl.ds(pl.multiple_of(part * part_rows, 8), part_rows)
        return pltpu.make_async_copy(
            f_ref.at[:, span, pl.ds(half * LANES, LANES)], out_ref.at[half, :, span, :], sems.at[part * 2 + half]
        )

    for part in range(PARTS):
        for half in range(2):
            copy(part, half).start()

    def tile(r):
        here = pl.ds(pl.multiple_of(r * 8, 8), 8)
        acc = jnp.zeros((8, LANES), jnp.float32)
        for k in range(depth):
            first = pltpu.roll(out_ref[0, k, here, :], k, 1) if k else out_ref[0, k, here, :]
            last = pltpu.roll(out_ref[1, k, here, :], depth + k + 1, 1)
            acc = jnp.where(lane == k, first, acc)
            acc = jnp.where(lane == depth + k, last, acc)
        packed[here, :] = acc

    def step(part, carry):
        for half in range(2):
            copy(part, half).wait()
        for r in range(part_rows // 8):
            tile(part * (part_rows // 8) + r)
        return carry

    lax.fori_loop(0, PARTS, step, 0)
    even_x, even_y = is_even("gx"), is_even("gy")
    turned = packed[...].T
    left, right = turned[0:depth], turned[depth : 2 * depth]
    x0_ref[...] = pick(even_x, right, left)
    x1_ref[...] = pick(even_x, left, right)
    for half in range(2):
        for k in range(depth):
            low, high = out_ref[half, k, 0:1, :], out_ref[half, k, rows - 1 : rows, :]
            y0_ref[half, pl.ds(k, 1), :] = pick(even_y, high, low)
            y1_ref[half, pl.ds(k, 1), :] = pick(even_y, low, high)


def faces(field):
    depth, rows, cols = field.shape
    vmem = pl.BlockSpec(memory_space=pltpu.VMEM)
    shapes = [(2, depth, rows, LANES)] + [(depth, rows)] * 2 + [(2, depth, LANES)] * 2
    return pl.pallas_call(
        face_kernel,
        in_specs=[pl.BlockSpec(memory_space=pl.ANY)],
        out_specs=[vmem] * 5,
        out_shape=[jax.ShapeDtypeStruct(shape, jnp.float32) for shape in shapes],
        scratch_shapes=[pltpu.VMEM((rows, LANES), jnp.float32), pltpu.SemaphoreType.DMA((2 * PARTS,))],
        compiler_params=pltpu.CompilerParams(vmem_limit_bytes=FACE_LIMIT),
    )(field)


def side_columns(x0_ref, x1_ref, mix, side_ref):
    depth = x0_ref.shape[0]
    even, end = is_even("gx"), at_end("gx")
    mix[...] = jnp.zeros_like(mix)
    for k in range(depth):
        first, second = x0_ref[pl.ds(k, 1), :], drop(end, x1_ref[pl.ds(k, 1), :])
        mix[pl.ds(2 * k, 1), :] = pick(even, second, first)
        mix[pl.ds((2 * k + LANES - 1) % LANES, 1), :] = pick(even, first, second)
    side_ref[...] = mix[...].T


def rim_rows(f_ref, y0_ref, y1_ref, rim):
    depth, rows = f_ref.shape[1:3]
    even, end = is_even("gy"), at_end("gy")
    for half in range(2):
        for k in range(depth):
            first, second = y0_ref[half, pl.ds(k, 1), :], drop(end, y1_ref[half, pl.ds(k, 1), :])
            rim[0, half, k, pl.ds(7, 1), :] = pick(even, second, first)
            rim[0, half, k, pl.ds(8, 16), :] = f_ref[half, k, pl.ds(0, 16), :]
            rim[1, half, k, pl.ds(0, 16), :] = f_ref[half, k, pl.ds(rows - 16, 16), :]
            rim[1, half, k, pl.ds(16, 1), :] = pick(even, first, second)


def march_tile(density, depth, r, source, offset, side_ref, z0_ref, z1_ref):
    base = pl.multiple_of(r * 8, 8)
    lane = lax.broadcasted_iota(jnp.int32, (8, LANES), 1)
    is_first = lane == 0
    is_last = lane == LANES - 1
    ext_scale = 4.0 * density * LOG2E
    ext_base = 1.2 * density * LOG2E
    even, end = is_even("gz"), at_end("gz")

    def load(half, k, up):
        return source[half, k, pl.ds(offset + up, 8), :]

    def depth_halo(half, near):
        here = pl.ds(base, 8), pl.ds(half * LANES, LANES)
        first = z0_ref[here]
        second = drop(end, z1_ref[here])
        return pick(even, second, first) if near else pick(even, first, second)

    packed = side_ref[pl.ds(base, 8), :]
    prev = [depth_halo(h, True) for h in range(2)]
    cur = [load(h, 0, 0) for h in range(2)]
    through = [jnp.ones((8, LANES), jnp.float32)] * 2
    total = [jnp.zeros((8, LANES), jnp.float32)] * 2
    tilted = [jnp.zeros((8, LANES), jnp.float32)] * 2
    bell = [jnp.zeros((8, LANES), jnp.float32)] * 2
    for k in range(depth):
        if k + 1 < depth:
            nxt = [load(h, k + 1, 0) for h in range(2)]
        else:
            nxt = [depth_halo(h, False) for h in range(2)]
        edge = pltpu.roll(packed, LANES - 2 * k, 1) if k else packed
        fwd = [pltpu.roll(c, LANES - 1, 1) for c in cur]
        bwd = [pltpu.roll(c, 1, 1) for c in cur]
        upper = [jnp.where(is_last, fwd[1], fwd[0]), jnp.where(is_last, edge, fwd[1])]
        lower = [jnp.where(is_first, edge, bwd[0]), jnp.where(is_first, bwd[0], bwd[1])]
        for h in range(2):
            f = cur[h]
            a = upper[h] - lower[h]
            b = load(h, k, 1) - load(h, k, -1)
            c = nxt[h] - prev[h]
            bc = b + c
            slope = jnp.abs((bc + bc) + a)
            inv = lax.rsqrt(((c * c + b * b) + 4.0) + a * a)
            t = jnp.tanh(f)
            gauss = jnp.exp2(f * (f * -LOG2E))
            keep = jnp.exp2((1.0 + t) * (inv * inv * ext_scale - ext_base))
            after = through[h] * keep
            w = through[h] - after
            ws = w * (1.0 + slope * inv)
            through[h] = after
            total[h] = total[h] + ws
            tilted[h] = tilted[h] + ws * t
            bell[h] = bell[h] + ws * gauss
        prev, cur = cur, nxt
    return [(total[h], tilted[h], bell[h], through[h]) for h in range(2)]


def first_kernel(density, f_ref, x0_ref, x1_ref, y0_ref, y1_ref, z0_ref, z1_ref, keep_ref, send_ref, side_ref, mix):
    depth = f_ref.shape[1]
    side_columns(x0_ref, x1_ref, mix, side_ref)
    even = is_even("gz")

    def step(band, carry):
        r = jnp.where(band == 0, 1, 2 * band)
        halves = march_tile(density, depth, r, f_ref, pl.multiple_of(r * 8, 8), side_ref, z0_ref, z1_ref)
        for c, (left, right) in enumerate(zip(*halves)):
            keep_ref[band, c] = pick(even, left, right)
            send_ref[band, c] = pick(even, right, left)
        return carry

    lax.fori_loop(0, BANDS, step, 0, unroll=4)


def rest_kernel(density, f_ref, side_ref, y0_ref, y1_ref, z0_ref, z1_ref, out_ref, rim):
    depth, rows = f_ref.shape[1:3]
    rim_rows(f_ref, y0_ref, y1_ref, rim)

    def tile(band, r, source, offset):
        halves = march_tile(density, depth, r, source, offset, side_ref, z0_ref, z1_ref)
        for half in range(2):
            for c in range(4):
                out_ref[band, half + 1, c] = halves[half][c]

    def step(band, carry):
        r = 2 * band + 1
        tile(band, r, f_ref, pl.multiple_of(r * 8, 8))
        return carry

    tile(0, jnp.int32(0), rim.at[0], 8)
    lax.fori_loop(1, BANDS - 1, step, 0, unroll=7)
    tile(BANDS - 1, jnp.int32(rows // 8 - 1), rim.at[1], 8)


def merge_kernel(own_ref, other_ref, parts_ref, out_ref):
    even = is_even("gz")

    def step(band, carry):
        mine = [own_ref[band, c] for c in range(4)]
        theirs = [other_ref[band, c] for c in range(4)]
        near = [pick(even, m, t) for m, t in zip(mine, theirs)]
        far = [pick(even, t, m) for m, t in zip(mine, theirs)]
        for c in range(3):
            out_ref[band, 0, c] = near[c] + near[3] * far[c]
        out_ref[band, 0, 3] = near[3] * far[3]
        return carry

    lax.fori_loop(0, BANDS, step, 0, unroll=4)


def call(kernel, shapes, scratch, args, cells=0, aliases={}):
    vmem = pl.BlockSpec(memory_space=pltpu.VMEM)
    cost = pl.CostEstimate(flops=40 * cells, bytes_accessed=4 * cells, transcendentals=4 * cells) if cells else None
    return pl.pallas_call(
        kernel,
        in_specs=[vmem] * len(args),
        out_specs=[vmem] * len(shapes),
        out_shape=[jax.ShapeDtypeStruct(shape, jnp.float32) for shape in shapes],
        scratch_shapes=scratch,
        input_output_aliases=aliases,
        cost_estimate=cost,
        compiler_params=pltpu.CompilerParams(vmem_limit_bytes=MARCH_LIMIT),
    )(*args)


def blend_kernel(parts_ref, out_ref):
    lone = lax.axis_index("gz") == 0
    for block, half, ids in (
        (0, 0, range(0, BANDS, 2)),
        (0, 1, range(1, BANDS, 2)),
        (1, 0, range(BANDS)),
        (2, 1, range(BANDS)),
    ):
        through = jnp.ones((8, LANES), jnp.float32)
        sums = [jnp.zeros((8, LANES), jnp.float32) for c in range(3)]
        for d in ids:
            for c in range(3):
                sums[c] = sums[c] + through * parts_ref[d, block, c]
            through = through * parts_ref[d, block, 3]
        where = jnp.where(lone, 8, 0) if block == 0 else jnp.where(lone, 0, 8)
        rows = pl.ds(pl.multiple_of(where, 8), 8)
        cols = pl.ds(half * LANES, LANES)
        out_ref[0, rows, cols] = (sums[0] + sums[1]) * 0.125
        out_ref[1, rows, cols] = sums[2] * 0.25
        out_ref[2, rows, cols] = (sums[0] - sums[1]) * 0.125
        out_ref[3, rows, cols] = 1.0 - through


def blend(parts, cols):
    return pl.pallas_call(
        blend_kernel,
        in_specs=[pl.BlockSpec(memory_space=pltpu.VMEM)],
        out_specs=pl.BlockSpec(memory_space=pltpu.VMEM),
        out_shape=jax.ShapeDtypeStruct((4, 16, cols), jnp.float32),
        compiler_params=pltpu.CompilerParams(vmem_limit_bytes=MARCH_LIMIT),
    )(parts)


def swap(block, axis, start):
    count = lax.axis_size(axis)
    pairs = []
    for i in range(start, count, 2):
        pairs += [(i, (i + 1) % count), ((i + 1) % count, i)]
    return lax.ppermute(block, axis, pairs)


def per_device(field):
    depth = field.shape[0]
    density = 4.0 / (depth * lax.axis_size("gz"))
    even = is_even("gz")
    z0 = swap(field[jnp.where(even, depth - 1, 0)], "gz", 0)
    z1 = swap(field[jnp.where(even, 0, depth - 1)], "gz", 1)
    whole, x0, x1, y0, y1 = faces(field)
    x0, x1 = swap(x0, "gx", 0), swap(x1, "gx", 1)
    y0, y1 = swap(y0, "gy", 0), swap(y1, "gy", 1)
    cells = depth * BANDS * 8 * field.shape[2]
    block = (BANDS, 4, 8, LANES)
    own, sent, side = call(
        functools.partial(first_kernel, density),
        [block, block, (BANDS * 16, LANES)],
        [pltpu.VMEM((LANES, BANDS * 16), jnp.float32)],
        (whole, x0, x1, y0, y1, z0, z1),
        cells,
    )
    other = swap(sent, "gz", 0)
    (parts,) = call(
        functools.partial(rest_kernel, density),
        [(BANDS, 3, 4, 8, LANES)],
        [pltpu.VMEM((2, 2, depth, 24, LANES), jnp.float32)],
        (whole, side, y0, y1, z0, z1),
        cells,
    )
    (parts,) = call(merge_kernel, [parts.shape], [], (own, other, parts), aliases={2: 0})
    parts = lax.all_to_all(parts, "gz", split_axis=0, concat_axis=0, tiled=True)
    return blend(parts, field.shape[2])


def solution(mesh):
    return jax.shard_map(
        per_device,
        mesh=mesh,
        in_specs=(P("gz", "gy", "gx"),),
        out_specs=P(None, ("gy", "gz"), "gx"),
        check_vma=False,
    )
```

```python
import functools

import jax
import jax.numpy as jnp
from jax import lax
from jax.experimental import pallas as pl
from jax.experimental.pallas import tpu as pltpu
from jax.sharding import PartitionSpec as P

LOG2E = 1.4426950408889634
LANES = 128
BANDS = 16
PARTS = 8
FACE_LIMIT = 40 * 1024 * 1024
MARCH_LIMIT = 24 * 1024 * 1024


def is_even(axis):
    return lax.rem(lax.axis_index(axis), 2) == 0


def at_end(axis):
    place = lax.axis_index(axis)
    return (place == 0) | (place == lax.axis_size(axis) - 1)


def drop(end, block):
    return jnp.where(jnp.broadcast_to(end, block.shape), 0.0, block)


def pick(even, yes, no):
    return jnp.where(jnp.broadcast_to(even, yes.shape), yes, no)


def face_kernel(f_ref, out_ref, x0_ref, x1_ref, y0_ref, y1_ref, packed, sems):
    depth, rows, cols = f_ref.shape
    part_rows = rows // PARTS
    lane = lax.broadcasted_iota(jnp.int32, (8, LANES), 1)

    def copy(part, half):
        span = pl.ds(pl.multiple_of(part * part_rows, 8), part_rows)
        return pltpu.make_async_copy(
            f_ref.at[:, span, pl.ds(half * LANES, LANES)], out_ref.at[half, :, span, :], sems.at[part * 2 + half]
        )

    for part in range(PARTS):
        for half in range(2):
            copy(part, half).start()

    def tile(r):
        here = pl.ds(pl.multiple_of(r * 8, 8), 8)
        acc = jnp.zeros((8, LANES), jnp.float32)
        for k in range(depth):
            first = pltpu.roll(out_ref[0, k, here, :], k, 1) if k else out_ref[0, k, here, :]
            last = pltpu.roll(out_ref[1, k, here, :], depth + k + 1, 1)
            acc = jnp.where(lane == k, first, acc)
            acc = jnp.where(lane == depth + k, last, acc)
        packed[here, :] = acc

    def step(part, carry):
        for half in range(2):
            copy(part, half).wait()
        for r in range(part_rows // 8):
            tile(part * (part_rows // 8) + r)
        return carry

    lax.fori_loop(0, PARTS, step, 0)
    even_x, even_y = is_even("gx"), is_even("gy")
    turned = packed[...].T
    left, right = turned[0:depth], turned[depth : 2 * depth]
    x0_ref[...] = pick(even_x, right, left)
    x1_ref[...] = pick(even_x, left, right)
    for half in range(2):
        for k in range(depth):
            low, high = out_ref[half, k, 0:1, :], out_ref[half, k, rows - 1 : rows, :]
            y0_ref[half, pl.ds(k, 1), :] = pick(even_y, high, low)
            y1_ref[half, pl.ds(k, 1), :] = pick(even_y, low, high)


def faces(field):
    depth, rows, cols = field.shape
    vmem = pl.BlockSpec(memory_space=pltpu.VMEM)
    shapes = [(2, depth, rows, LANES)] + [(depth, rows)] * 2 + [(2, depth, LANES)] * 2
    return pl.pallas_call(
        face_kernel,
        in_specs=[pl.BlockSpec(memory_space=pl.ANY)],
        out_specs=[vmem] * 5,
        out_shape=[jax.ShapeDtypeStruct(shape, jnp.float32) for shape in shapes],
        scratch_shapes=[pltpu.VMEM((rows, LANES), jnp.float32), pltpu.SemaphoreType.DMA((2 * PARTS,))],
        compiler_params=pltpu.CompilerParams(vmem_limit_bytes=FACE_LIMIT),
    )(field)


def side_columns(x0_ref, x1_ref, mix, side_ref):
    depth = x0_ref.shape[0]
    even, end = is_even("gx"), at_end("gx")
    mix[...] = jnp.zeros_like(mix)
    for k in range(depth):
        first, second = x0_ref[pl.ds(k, 1), :], drop(end, x1_ref[pl.ds(k, 1), :])
        mix[pl.ds(2 * k, 1), :] = pick(even, second, first)
        mix[pl.ds((2 * k + LANES - 1) % LANES, 1), :] = pick(even, first, second)
    side_ref[...] = mix[...].T


def rim_rows(f_ref, y0_ref, y1_ref, rim):
    depth, rows = f_ref.shape[1:3]
    even, end = is_even("gy"), at_end("gy")
    for half in range(2):
        for k in range(depth):
            first, second = y0_ref[half, pl.ds(k, 1), :], drop(end, y1_ref[half, pl.ds(k, 1), :])
            rim[0, half, k, pl.ds(7, 1), :] = pick(even, second, first)
            rim[0, half, k, pl.ds(8, 16), :] = f_ref[half, k, pl.ds(0, 16), :]
            rim[1, half, k, pl.ds(0, 16), :] = f_ref[half, k, pl.ds(rows - 16, 16), :]
            rim[1, half, k, pl.ds(16, 1), :] = pick(even, first, second)


def march_tile(density, depth, r, source, offset, side_ref, z0_ref, z1_ref):
    base = pl.multiple_of(r * 8, 8)
    lane = lax.broadcasted_iota(jnp.int32, (8, LANES), 1)
    is_first = lane == 0
    is_last = lane == LANES - 1
    ext_scale = 4.0 * density * LOG2E
    ext_base = 1.2 * density * LOG2E
    even, end = is_even("gz"), at_end("gz")

    def load(half, k, up):
        return source[half, k, pl.ds(offset + up, 8), :]

    def depth_halo(half, near):
        here = pl.ds(base, 8), pl.ds(half * LANES, LANES)
        first = z0_ref[here]
        second = drop(end, z1_ref[here])
        return pick(even, second, first) if near else pick(even, first, second)

    packed = side_ref[pl.ds(base, 8), :]
    prev = [depth_halo(h, True) for h in range(2)]
    cur = [load(h, 0, 0) for h in range(2)]
    through = [jnp.ones((8, LANES), jnp.float32)] * 2
    total = [jnp.zeros((8, LANES), jnp.float32)] * 2
    tilted = [jnp.zeros((8, LANES), jnp.float32)] * 2
    bell = [jnp.zeros((8, LANES), jnp.float32)] * 2
    for k in range(depth):
        if k + 1 < depth:
            nxt = [load(h, k + 1, 0) for h in range(2)]
        else:
            nxt = [depth_halo(h, False) for h in range(2)]
        edge = pltpu.roll(packed, LANES - 2 * k, 1) if k else packed
        fwd = [pltpu.roll(c, LANES - 1, 1) for c in cur]
        bwd = [pltpu.roll(c, 1, 1) for c in cur]
        upper = [jnp.where(is_last, fwd[1], fwd[0]), jnp.where(is_last, edge, fwd[1])]
        lower = [jnp.where(is_first, edge, bwd[0]), jnp.where(is_first, bwd[0], bwd[1])]
        for h in range(2):
            f = cur[h]
            a = upper[h] - lower[h]
            b = load(h, k, 1) - load(h, k, -1)
            c = nxt[h] - prev[h]
            bc = b + c
            slope = jnp.abs((bc + bc) + a)
            inv = lax.rsqrt(((c * c + b * b) + 4.0) + a * a)
            t = jnp.tanh(f)
            gauss = jnp.exp2(f * (f * -LOG2E))
            keep = jnp.exp2((1.0 + t) * (inv * inv * ext_scale - ext_base))
            after = through[h] * keep
            w = through[h] - after
            ws = w * (1.0 + slope * inv)
            through[h] = after
            total[h] = total[h] + ws
            tilted[h] = tilted[h] + ws * t
            bell[h] = bell[h] + ws * gauss
        prev, cur = cur, nxt
    return [(total[h], tilted[h], bell[h], through[h]) for h in range(2)]


def first_kernel(density, f_ref, x0_ref, x1_ref, y0_ref, y1_ref, z0_ref, z1_ref, keep_ref, send_ref, side_ref, mix):
    depth = f_ref.shape[1]
    side_columns(x0_ref, x1_ref, mix, side_ref)
    even = is_even("gz")

    def step(band, carry):
        r = jnp.where(band == 0, 1, 2 * band)
        halves = march_tile(density, depth, r, f_ref, pl.multiple_of(r * 8, 8), side_ref, z0_ref, z1_ref)
        for c, (left, right) in enumerate(zip(*halves)):
            keep_ref[band, c] = pick(even, left, right)
            send_ref[band, c] = pick(even, right, left)
        return carry

    lax.fori_loop(0, BANDS, step, 0, unroll=8)


def rest_kernel(density, f_ref, side_ref, y0_ref, y1_ref, z0_ref, z1_ref, out_ref, rim):
    depth, rows = f_ref.shape[1:3]
    rim_rows(f_ref, y0_ref, y1_ref, rim)

    def tile(band, r, source, offset):
        halves = march_tile(density, depth, r, source, offset, side_ref, z0_ref, z1_ref)
        for half in range(2):
            for c in range(4):
                out_ref[band, half + 1, c] = halves[half][c]

    def step(band, carry):
        r = 2 * band + 1
        tile(band, r, f_ref, pl.multiple_of(r * 8, 8))
        return carry

    tile(0, jnp.int32(0), rim.at[0], 8)
    lax.fori_loop(1, BANDS - 1, step, 0, unroll=7)
    tile(BANDS - 1, jnp.int32(rows // 8 - 1), rim.at[1], 8)


def merge_kernel(own_ref, other_ref, parts_ref, out_ref):
    even = is_even("gz")

    def step(band, carry):
        mine = [own_ref[band, c] for c in range(4)]
        theirs = [other_ref[band, c] for c in range(4)]
        near = [pick(even, m, t) for m, t in zip(mine, theirs)]
        far = [pick(even, t, m) for m, t in zip(mine, theirs)]
        for c in range(3):
            out_ref[band, 0, c] = near[c] + near[3] * far[c]
        out_ref[band, 0, 3] = near[3] * far[3]
        return carry

    lax.fori_loop(0, BANDS, step, 0, unroll=4)


def call(kernel, shapes, scratch, args, cells=0, aliases={}):
    vmem = pl.BlockSpec(memory_space=pltpu.VMEM)
    cost = pl.CostEstimate(flops=40 * cells, bytes_accessed=4 * cells, transcendentals=4 * cells) if cells else None
    return pl.pallas_call(
        kernel,
        in_specs=[vmem] * len(args),
        out_specs=[vmem] * len(shapes),
        out_shape=[jax.ShapeDtypeStruct(shape, jnp.float32) for shape in shapes],
        scratch_shapes=scratch,
        input_output_aliases=aliases,
        cost_estimate=cost,
        compiler_params=pltpu.CompilerParams(vmem_limit_bytes=MARCH_LIMIT),
    )(*args)


def blend_kernel(parts_ref, out_ref):
    lone = lax.axis_index("gz") == 0
    for block, half, ids in (
        (0, 0, range(0, BANDS, 2)),
        (0, 1, range(1, BANDS, 2)),
        (1, 0, range(BANDS)),
        (2, 1, range(BANDS)),
    ):
        through = jnp.ones((8, LANES), jnp.float32)
        sums = [jnp.zeros((8, LANES), jnp.float32) for c in range(3)]
        for d in ids:
            for c in range(3):
                sums[c] = sums[c] + through * parts_ref[d, block, c]
            through = through * parts_ref[d, block, 3]
        where = jnp.where(lone, 8, 0) if block == 0 else jnp.where(lone, 0, 8)
        rows = pl.ds(pl.multiple_of(where, 8), 8)
        cols = pl.ds(half * LANES, LANES)
        out_ref[0, rows, cols] = (sums[0] + sums[1]) * 0.125
        out_ref[1, rows, cols] = sums[2] * 0.25
        out_ref[2, rows, cols] = (sums[0] - sums[1]) * 0.125
        out_ref[3, rows, cols] = 1.0 - through


def blend(parts, cols):
    return pl.pallas_call(
        blend_kernel,
        in_specs=[pl.BlockSpec(memory_space=pltpu.VMEM)],
        out_specs=pl.BlockSpec(memory_space=pltpu.VMEM),
        out_shape=jax.ShapeDtypeStruct((4, 16, cols), jnp.float32),
        compiler_params=pltpu.CompilerParams(vmem_limit_bytes=MARCH_LIMIT),
    )(parts)


def swap(block, axis, start):
    count = lax.axis_size(axis)
    pairs = []
    for i in range(start, count, 2):
        pairs += [(i, (i + 1) % count), ((i + 1) % count, i)]
    return lax.ppermute(block, axis, pairs)


def per_device(field):
    depth = field.shape[0]
    density = 4.0 / (depth * lax.axis_size("gz"))
    even = is_even("gz")
    z0 = swap(field[jnp.where(even, depth - 1, 0)], "gz", 0)
    z1 = swap(field[jnp.where(even, 0, depth - 1)], "gz", 1)
    whole, x0, x1, y0, y1 = faces(field)
    x0, x1 = swap(x0, "gx", 0), swap(x1, "gx", 1)
    y0, y1 = swap(y0, "gy", 0), swap(y1, "gy", 1)
    cells = depth * BANDS * 8 * field.shape[2]
    block = (BANDS, 4, 8, LANES)
    own, sent, side = call(
        functools.partial(first_kernel, density),
        [block, block, (BANDS * 16, LANES)],
        [pltpu.VMEM((LANES, BANDS * 16), jnp.float32)],
        (whole, x0, x1, y0, y1, z0, z1),
        cells,
    )
    other = swap(sent, "gz", 0)
    (parts,) = call(
        functools.partial(rest_kernel, density),
        [(BANDS, 3, 4, 8, LANES)],
        [pltpu.VMEM((2, 2, depth, 24, LANES), jnp.float32)],
        (whole, side, y0, y1, z0, z1),
        cells,
    )
    (parts,) = call(merge_kernel, [parts.shape], [], (own, other, parts), aliases={2: 0})
    parts = lax.all_to_all(parts, "gz", split_axis=0, concat_axis=0, tiled=True)
    return blend(parts, field.shape[2])


def solution(mesh):
    return jax.shard_map(
        per_device,
        mesh=mesh,
        in_specs=(P("gz", "gy", "gx"),),
        out_specs=P(None, ("gy", "gz"), "gx"),
        check_vma=False,
    )
```
